32 devices in a mesh: seq: 8 (over z, x), chan: 4 (over y, core).
Axes of the slice: x: 2, y: 2, z: 4, core: 2. Of those that a mesh axis runs over, the one named last changes fastest.
Arguments:
- projected: bfloat16 [3, 64, 524288], P(None, None, ('seq', 'chan')), may hold values from -6 to 6
- live_blocks: int32 [4096], P('seq'), may hold values 0 or 1
- filters: float32 [4, 524288], P('chan', 'seq'), as said below
- skip_gain: float32 [64], P('chan'), may hold values from -2 to 2
Outputs:
- gated: bfloat16 [64, 524288], P('chan', 'seq')
The draws below stay inside these ranges and needn't reach their ends.
Inputs may be any that keep to these rules, and one draw needn't show every extreme that they name: filters holds finite float32 taps.
All inputs are finite; a program needn't handle non-finite values. No bound on the sum of `live_blocks` on one device may be relied on, other than what follows from the above.
Results may differ from the reference program's by a relative error of at most 0.0049.
Values may be sent and summed in bfloat16 or wider, within the bound.
A program may use at most 256 MiB of HBM per device.

```python
import math
import jax
import jax.numpy as jnp
from jax import lax

C = 64
GROUP = 16
R = 128
N = 1048576
L = 524288
G = 4


def draw_filters(key, part):
    key = jax.random.fold_in(key, 11)
    first_key, second_key = jax.random.split(key, 2)
    taps = jnp.arange(L, dtype=jnp.float32)
    order = jnp.arange(G, dtype=jnp.float32)
    spread = (order + jax.random.uniform(first_key, (G,), jnp.float32)) / G
    reach = L * jnp.exp(-math.log(16.0) * spread)
    slow_part = jnp.exp(-taps[None, :] / reach[:, None]) * jnp.sqrt(2.0 / reach)[:, None]
    fast_part = 0.5 * jnp.exp(-taps / 16.0)
    envelope = fast_part[None, :] + slow_part
    noise = jax.random.normal(second_key, (G, L), jnp.float32)
    return (noise * envelope).astype(jnp.float32)


def touch_ends(array, own_key, smallest, high):
    place = [jax.random.randint(jax.random.fold_in(own_key, axis), (), 0, length) for axis, length in enumerate(array.shape)]
    longest = array.shape.index(max(array.shape))
    beside = place[:longest] + [(place[longest] + 1) % array.shape[longest]] + place[longest + 1:]
    return array.at[tuple(place)].set(smallest).at[tuple(beside)].set(high)


def levels(key, shape, cuts, least, largest):
    def one(position, blocks):
        steps = jax.random.uniform(jax.random.fold_in(jax.random.fold_in(key, 6), position), (blocks,), jnp.float32, least / len(cuts), largest / len(cuts))
        return jnp.repeat(jnp.exp(steps), shape[position] // blocks).reshape((-1,) + (1,) * (len(shape) - position - 1))

    gain = one(*cuts[0])
    for cut in cuts[1:]:
        gain = gain * one(*cut)
    return gain


def scatter_about(rng, extent, deviation, most, cuts=(), kind=jnp.bfloat16):
    factor_of = levels(rng, extent, cuts, -0.22, 0.18) if cuts else 1.0
    values = jax.random.normal(rng, extent, jnp.float32) * deviation * factor_of
    return jnp.minimum(jnp.maximum(values, -most), most).astype(kind)


def setup_inputs(seed: int = 0) -> dict:
    streams_of = jax.random.split(jax.random.key(seed), 5)
    projected = scatter_about(streams_of[0], (3, C, L), 1.0, 6.0, ((2, 32),))
    live_blocks = touch_ends((jax.random.randint(streams_of[1], (L // R,), 0, 4) < 3).astype(jnp.int32), jax.random.fold_in(streams_of[1], 1), 0, 1)
    filters = draw_filters(jax.random.fold_in(streams_of[4], 71), 0)
    skip_gain = scatter_about(streams_of[3], (C,), 0.5, 2.0, ((0, 4),), jnp.float32)
    return {"projected": projected, "live_blocks": live_blocks, "filters": filters, "skip_gain": skip_gain}


def reference(projected, live_blocks, filters, skip_gain):
    gate_rows = projected[0].astype(jnp.float32)
    key_rows = projected[1].astype(jnp.float32)
    value_rows = projected[2].astype(jnp.float32)
    keep_mask = jnp.broadcast_to(live_blocks[:, None], (L // R, R)).reshape(L).astype(jnp.float32)
    product_rows = (key_rows * value_rows * keep_mask[None, :]).astype(jnp.bfloat16)

    def one_group(group_id):
        channel_rows = lax.dynamic_slice_in_dim(product_rows, group_id * GROUP, GROUP, 0).astype(jnp.float32)
        filter_row = lax.dynamic_slice_in_dim(filters, group_id, 1, 0)
        filter_spec = jnp.fft.rfft(filter_row, n=N, axis=-1)
        spectra = jnp.fft.rfft(channel_rows, n=N, axis=-1)
        filtered = spectra * filter_spec
        convolved = jnp.fft.irfft(filtered, n=N, axis=-1)[:, :L]
        return convolved.astype(jnp.float32)

    convolved = lax.map(one_group, jnp.arange(G, dtype=jnp.int32)).reshape(C, L)
    direct = skip_gain[:, None] * product_rows.astype(jnp.float32)
    return (gate_rows * (convolved + direct)).astype(jnp.bfloat16)
```

```python
import math

import jax
import jax.numpy as jnp
import numpy as np
from jax import lax
from jax.sharding import PartitionSpec as P

P1 = 128
HALF = 64
Q = 64
R = 128
N = P1 * Q * R


def roots(exponent, total):
    angles = 2.0 * math.pi / total * (np.asarray(exponent, np.int64) % total)
    return np.cos(angles), -np.sin(angles)


def tables():
    k1, n1 = np.arange(P1), np.arange(HALF)
    k2, n3 = np.arange(Q), np.arange(R)
    fr, fi = roots(np.outer(k1, n1), P1)
    first = np.block([[fr, -fi], [fi, fr]])
    last = np.block([[fr.T, fi.T], [-fi.T, fr.T]]) / N
    tr, ti = roots(np.outer(k1, k2), P1 * Q)
    sr, si = roots(np.outer(k2, k2), Q)
    cr, ci = roots(np.outer(n3, n3), R)
    ar, ai = roots(np.outer(k1, n3), N)
    br, bi = roots(np.outer(k2, n3), Q * R)
    return [
        np.asarray(t, np.float32) for t in (first, last, tr, ti, sr, si, cr, ci, ar, ai, br, bi)
    ]


def dot(form, a, b):
    return jnp.einsum(form, a, b, precision=lax.Precision.HIGHEST)


def turn(re, im, c, s):
    return re * c - im * s, re * s + im * c


def forward(first, parts, tabs):
    _, _, tr, ti, sr, si, cr, ci, wr, wi = tabs
    flat = dot("kn,nm->km", first, parts)
    re, im = flat[:P1].reshape(P1, Q, R), flat[P1:].reshape(P1, Q, R)
    re, im = turn(re, im, tr[:, :, None], ti[:, :, None])
    re, im = (
        dot("kn,pnr->pkr", sr, re) - dot("kn,pnr->pkr", si, im),
        dot("kn,pnr->pkr", sr, im) + dot("kn,pnr->pkr", si, re),
    )
    re, im = turn(re, im, wr, wi)
    return (
        dot("pqr,rk->pqk", re, cr) - dot("pqr,rk->pqk", im, ci),
        dot("pqr,rk->pqk", im, cr) + dot("pqr,rk->pqk", re, ci),
    )


def backward(re, im, tabs):
    _, last, tr, ti, sr, si, cr, ci, wr, wi = tabs
    re, im = (
        dot("pqr,rk->pqk", re, cr) + dot("pqr,rk->pqk", im, ci),
        dot("pqr,rk->pqk", im, cr) - dot("pqr,rk->pqk", re, ci),
    )
    re, im = turn(re, im, wr, -wi)
    re, im = (
        dot("kn,pnr->pkr", sr, re) + dot("kn,pnr->pkr", si, im),
        dot("kn,pnr->pkr", sr, im) - dot("kn,pnr->pkr", si, re),
    )
    re, im = turn(re, im, tr[:, :, None], -ti[:, :, None])
    flat = jnp.concatenate([re, im], 0).reshape(2 * P1, Q * R)
    return dot("kn,nm->km", last, flat)


def body(projected, live_blocks, filters, skip_gain):
    seq, chan = lax.axis_size("seq"), lax.axis_size("chan")
    at_seq, at_chan = lax.axis_index("seq"), lax.axis_index("chan")
    channels, here = projected.shape[1], projected.shape[2]
    own = channels // chan
    pairs = own // 2
    copies = seq // pairs
    sub = live_blocks.shape[0] // chan
    span = here * chan
    keep = lax.dynamic_slice_in_dim(live_blocks, at_chan * sub, sub).astype(jnp.float32)
    keep = jnp.broadcast_to(keep[:, None], (sub, R)).reshape(1, here)
    product = (
        projected[1].astype(jnp.float32) * projected[2].astype(jnp.float32) * keep
    ).astype(jnp.bfloat16)
    rows = product.reshape(chan, pairs, 2, here // R, R)
    rows = jnp.repeat(rows, copies, axis=1) if copies > 1 else rows
    rows = rows.transpose(1, 0, 2, 3, 4).reshape(seq * chan, 2, here // R, R)
    rows = lax.all_to_all(rows, ("seq", "chan"), split_axis=0, concat_axis=0, tiled=True)
    taps = lax.all_gather(filters, "seq", axis=1, tiled=True)
    gate = lax.all_to_all(projected[0], "chan", split_axis=0, concat_axis=1, tiled=True)
    first, last, tr, ti, sr, si, cr, ci, ar, ai, br, bi = tables()
    wr, wi = turn(ar[:, None, :], ai[:, None, :], br[None], bi[None])
    tabs = (first, last, tr, ti, sr, si, cr, ci, wr, wi)
    signal = rows.transpose(1, 0, 2, 3).reshape(2 * HALF, Q * R).astype(jnp.float32)
    hr, hi = forward(first[:, :HALF], taps.reshape(HALF, Q * R), tabs)
    re, im = forward(first, signal, tabs)
    re, im = turn(re, im, hr, hi)
    convolved = backward(re, im, tabs)
    pair = at_seq // copies
    gain = lax.dynamic_slice_in_dim(skip_gain, 2 * pair, 2)
    gain = jnp.repeat(gain, HALF)[:, None]
    summed = (convolved + gain * signal).astype(jnp.bfloat16)
    summed = summed.reshape(2, seq, span // R, R).transpose(1, 0, 2, 3)
    summed = lax.all_to_all(summed, "seq", split_axis=0, concat_axis=0, tiled=True)
    summed = summed[::copies].reshape(own, span)
    return (gate.astype(jnp.float32) * summed.astype(jnp.float32)).astype(jnp.bfloat16)


def solution(mesh):
    in_specs = (P(None, None, ("seq", "chan")), P("seq"), P("chan", "seq"), P("chan"))
    out_specs = P("chan", "seq")
    return jax.shard_map(body, mesh=mesh, in_specs=in_specs, out_specs=out_specs, check_vma=False)
```

```python
import math

import jax
import jax.numpy as jnp
import numpy as np
from jax import lax
from jax.experimental import pallas as pl
from jax.experimental.pallas import tpu as pltpu
from jax.sharding import PartitionSpec as P

P1 = 128
HALF = 64
Q = 64
R = 128
N = P1 * Q * R


def roots(exponent, total):
    angles = 2.0 * math.pi / total * (np.asarray(exponent, np.int64) % total)
    return np.cos(angles), -np.sin(angles)


def halves(matrix):
    high = np.asarray(matrix, np.float32).astype(jnp.bfloat16)
    low = (np.asarray(matrix) - high.astype(np.float64)).astype(jnp.bfloat16)
    return high, low


def thrice(matrix, axis):
    high, low = halves(matrix)
    return np.concatenate([high, high, low], axis)


def tables():
    k1, n1 = np.arange(P1), np.arange(HALF)
    k2, n3 = np.arange(Q), np.arange(R)
    fr, fi = roots(np.outer(k1, n1), P1)
    sr, si = roots(np.outer(k2, k2), Q)
    cr, ci = roots(np.outer(n3, n3), R)
    ar, ai = roots(np.outer(k1, n3), N)
    gr, gi = roots(np.outer(k1, np.ones(R, np.int64)), P1 * Q)
    br, bi = roots(np.outer(k2, n3), Q * R)
    return {
        "first": np.concatenate(halves(np.block([[fr, -fi], [fi, fr]])), 1),
        "taps": thrice(np.concatenate([fr, fi], 0), 1),
        "last": thrice(np.block([[fr.T, fi.T], [-fi.T, fr.T]]) / N, 1),
        "second": thrice(np.concatenate([sr, si], 0), 1),
        "second_back": thrice(np.concatenate([sr, -si], 0), 1),
        "third": thrice(np.block([[cr, ci], [-ci, cr]]), 0),
        "third_back": thrice(np.block([[cr, -ci], [ci, cr]]), 0),
        "start": np.stack([ar, ai]).astype(np.float32),
        "step": np.stack([gr, gi]).astype(np.float32),
        "outer": np.stack([br, bi]).astype(np.float32),
    }


def turn(re, im, c, s):
    return re * c - im * s, re * s + im * c


def split(x, axis):
    high = x.astype(jnp.bfloat16)
    low = (x - high.astype(jnp.float32)).astype(jnp.bfloat16)
    return jnp.concatenate([high, low, high], axis)


def dot(a, b):
    return jnp.dot(a, b, preferred_element_type=jnp.float32)


WIDE = 4
ROWS = 4


def columns(step):
    return pl.ds(pl.multiple_of(step * WIDE * R, WIDE * R), WIDE * R)


def first_section(load, mat_ref, start_ref, step_ref, out_ref):
    def one(step, carry):
        wr, wi = carry
        flat = dot(mat_ref[...], load(step))
        for part in range(WIDE):
            piece = flat[:, part * R : (part + 1) * R]
            re, im = turn(piece[:P1], piece[P1:], wr, wi)
            where = pl.ds(step * WIDE + part, P1, stride=Q)
            out_ref[0, where, :] = re
            out_ref[1, where, :] = im
            wr, wi = turn(wr, wi, step_ref[0], step_ref[1])
        return wr, wi

    lax.fori_loop(0, Q // WIDE, one, (start_ref[0], start_ref[1]))


def middle(mat_ref, pieces):
    data = jnp.concatenate([x for piece in pieces for x in piece], 1)
    flat = dot(mat_ref[...], split(data, 0))
    done = []
    for part in range(len(pieces)):
        low = flat[:, 2 * part * R : (2 * part + 1) * R]
        high = flat[:, (2 * part + 1) * R : (2 * part + 2) * R]
        done.append((low[:Q] - high[Q:], high[:Q] + low[Q:]))
    return done


def lanes(pieces):
    return jnp.concatenate([jnp.concatenate(piece, 1) for piece in pieces], 0)


def later_sections(src_ref, step, second_ref, third_ref, outer_ref):
    pieces = []
    for part in range(ROWS):
        where = pl.ds(pl.multiple_of((step * ROWS + part) * Q, Q), Q)
        pieces.append((src_ref[0, where, :], src_ref[1, where, :]))
    pieces = middle(second_ref, pieces)
    pieces = [turn(re, im, outer_ref[0], outer_ref[1]) for re, im in pieces]
    return dot(split(lanes(pieces), 1), third_ref[...])


def block(step):
    return pl.ds(pl.multiple_of(step * ROWS * Q, ROWS * Q), ROWS * Q)


def taps_kernel(
    taps_ref, mat_ref, start_ref, step_ref, second_ref, third_ref, outer_ref, out_ref, held
):
    def load(step):
        return split(taps_ref[:, columns(step)], 0)

    first_section(load, mat_ref, start_ref, step_ref, held)

    def one(step, carry):
        flat = later_sections(held, step, second_ref, third_ref, outer_ref)
        out_ref[0, block(step), :] = flat[:, :R]
        out_ref[1, block(step), :] = flat[:, R:]
        return carry

    lax.fori_loop(0, P1 // ROWS, one, 0)


def signal_kernel(
    signal_ref,
    spectrum_ref,
    gain_ref,
    mat_ref,
    last_ref,
    start_ref,
    step_ref,
    second_ref,
    back_ref,
    third_ref,
    third_back_ref,
    outer_ref,
    out_ref,
    held,
):
    def load(step):
        part = signal_ref[:, columns(step)]
        return jnp.concatenate([part, part], 0)

    first_section(load, mat_ref, start_ref, step_ref, held)

    def one(step, carry):
        flat = later_sections(held, step, second_ref, third_ref, outer_ref)
        re, im = turn(
            flat[:, :R], flat[:, R:], spectrum_ref[0, block(step), :], spectrum_ref[1, block(step), :]
        )
        flat = dot(split(jnp.concatenate([re, im], 1), 1), third_back_ref[...])
        pieces = []
        for part in range(ROWS):
            piece = flat[part * Q : (part + 1) * Q]
            pieces.append(turn(piece[:, :R], piece[:, R:], outer_ref[0], -outer_ref[1]))
        pieces = middle(back_ref, pieces)
        for part in range(ROWS):
            where = pl.ds(pl.multiple_of((step * ROWS + part) * Q, Q), Q)
            held[0, where, :] = pieces[part][0]
            held[1, where, :] = pieces[part][1]
        return carry

    lax.fori_loop(0, P1 // ROWS, one, 0)

    def finish(step, carry):
        wr, wi = carry
        found = []
        for part in range(WIDE):
            where = pl.ds(step * WIDE + part, P1, stride=Q)
            re, im = turn(held[0, where, :], held[1, where, :], wr, -wi)
            found.append(jnp.concatenate([re, im], 0))
            wr, wi = turn(wr, wi, step_ref[0], step_ref[1])
        flat = dot(last_ref[...], split(jnp.concatenate(found, 1), 0))
        direct = gain_ref[...] * signal_ref[:, columns(step)].astype(jnp.float32)
        out_ref[:, columns(step)] = (flat + direct).astype(jnp.bfloat16)
        return wr, wi

    lax.fori_loop(0, Q // WIDE, finish, (start_ref[0], start_ref[1]))


def run(kernel, out_shape, out_dtype, flops, *operands):
    return pl.pallas_call(
        kernel,
        out_shape=jax.ShapeDtypeStruct(out_shape, out_dtype),
        in_specs=[pl.BlockSpec(memory_space=pltpu.VMEM)] * len(operands),
        out_specs=pl.BlockSpec(memory_space=pltpu.VMEM),
        scratch_shapes=[pltpu.VMEM((2, P1 * Q, R), jnp.float32)],
        compiler_params=pltpu.CompilerParams(vmem_limit_bytes=52 * 1024 * 1024),
        cost_estimate=pl.CostEstimate(
            flops=flops, bytes_accessed=16 * 1024 * 1024, transcendentals=0
        ),
    )(*operands)


def transform_taps(taps, tabs):
    names = ("taps", "start", "step", "second", "third", "outer")
    return run(
        taps_kernel, (2, P1 * Q, R), jnp.float32, 10**10, taps, *[tabs[name] for name in names]
    )


def convolve(signal, spectrum, gain, tabs):
    names = (
        "first",
        "last",
        "start",
        "step",
        "second",
        "second_back",
        "third",
        "third_back",
        "outer",
    )
    operands = [tabs[name] for name in names]
    return run(
        signal_kernel,
        (2 * HALF, Q * R),
        jnp.bfloat16,
        2 * 10**10,
        signal,
        spectrum,
        gain,
        *operands,
    )


def body(projected, live_blocks, filters, skip_gain):
    seq, chan = lax.axis_size("seq"), lax.axis_size("chan")
    at_seq, at_chan = lax.axis_index("seq"), lax.axis_index("chan")
    channels, here = projected.shape[1], projected.shape[2]
    own = channels // chan
    pairs = own // 2
    copies = seq // pairs
    sub = live_blocks.shape[0] // chan
    span = here * chan
    keep = lax.dynamic_slice_in_dim(live_blocks, at_chan * sub, sub).astype(jnp.float32)
    keep = jnp.broadcast_to(keep[:, None], (sub, R)).reshape(1, here)
    product = (
        projected[1].astype(jnp.float32) * projected[2].astype(jnp.float32) * keep
    ).astype(jnp.bfloat16)
    rows = product.reshape(chan, pairs, 2, here // R, R)
    rows = jnp.repeat(rows, copies, axis=1) if copies > 1 else rows
    rows = rows.transpose(1, 0, 2, 3, 4).reshape(seq * chan, 2, here // R, R)
    rows = lax.all_to_all(rows, ("seq", "chan"), split_axis=0, concat_axis=0, tiled=True)
    taps = lax.all_gather(filters, "seq", axis=1, tiled=True)
    gate = lax.all_to_all(projected[0], "chan", split_axis=0, concat_axis=1, tiled=True)
    tabs = {name: jnp.asarray(table) for name, table in tables().items()}
    signal = rows.transpose(1, 0, 2, 3).reshape(2 * HALF, Q * R)
    spectrum = transform_taps(taps.reshape(HALF, Q * R), tabs)
    pair = at_seq // copies
    gain = lax.dynamic_slice_in_dim(skip_gain, 2 * pair, 2)
    gain = jnp.repeat(gain, HALF)[:, None]
    summed = convolve(signal, spectrum, gain, tabs)
    summed = summed.reshape(2, seq, span // R, R).transpose(1, 0, 2, 3)
    summed = lax.all_to_all(summed, "seq", split_axis=0, concat_axis=0, tiled=True)
    summed = summed[::copies].reshape(own, span)
    return (gate.astype(jnp.float32) * summed.astype(jnp.float32)).astype(jnp.bfloat16)


def solution(mesh):
    in_specs = (P(None, None, ("seq", "chan")), P("seq"), P("chan", "seq"), P("chan"))
    out_specs = P("chan", "seq")
    return jax.shard_map(body, mesh=mesh, in_specs=in_specs, out_specs=out_specs, check_vma=False)
```

```python
import math

import jax
import jax.numpy as jnp
import numpy as np
from jax import lax
from jax.experimental import pallas as pl
from jax.experimental.pallas import tpu as pltpu
from jax.sharding import PartitionSpec as P

P1 = 128
HALF = 64
Q = 64
R = 128
N = P1 * Q * R


def roots(exponent, total):
    angles = 2.0 * math.pi / total * (np.asarray(exponent, np.int64) % total)
    return np.cos(angles), -np.sin(angles)


def halves(matrix):
    high = np.asarray(matrix, np.float32).astype(jnp.bfloat16)
    low = (np.asarray(matrix) - high.astype(np.float64)).astype(jnp.bfloat16)
    return high, low


def thrice(matrix, axis):
    high, low = halves(matrix)
    return np.concatenate([high, high, low], axis)


def tables():
    k1, n1 = np.arange(P1), np.arange(HALF)
    k2, n3 = np.arange(Q), np.arange(R)
    fr, fi = roots(np.outer(k1, n1), P1)
    sr, si = roots(np.outer(k2, k2), Q)
    cr, ci = roots(np.outer(n3, n3), R)
    ar, ai = roots(np.outer(k1, n3), N)
    gr, gi = roots(np.outer(k1, np.ones(R, np.int64)), P1 * Q)
    br, bi = roots(np.outer(k2, n3), Q * R)
    return {
        "first": np.concatenate(halves(np.block([[fr, -fi], [fi, fr]])), 1),
        "taps": np.concatenate(halves(np.concatenate([fr, fi], 0)), 1),
        "last": thrice(np.block([[fr.T, fi.T], [-fi.T, fr.T]]) / N, 1),
        "second": thrice(np.concatenate([sr, si], 0), 1),
        "second_back": thrice(np.concatenate([sr, -si], 0), 1),
        "third": thrice(np.block([[cr, ci], [-ci, cr]]), 0),
        "third_short": np.concatenate(halves(np.block([[cr, ci], [-ci, cr]])), 0),
        "third_back": np.concatenate(halves(np.block([[cr, -ci], [ci, cr]])), 0),
        "start": np.stack([ar, ai]).astype(np.float32),
        "step": np.stack([gr, gi]).astype(np.float32),
        "outer": np.stack([br, bi]).astype(np.float32),
    }


def turn(re, im, c, s):
    return re * c - im * s, re * s + im * c


def split(x, axis):
    high = x.astype(jnp.bfloat16)
    low = (x - high.astype(jnp.float32)).astype(jnp.bfloat16)
    return jnp.concatenate([high, low, high], axis)


def twice(x, axis):
    high = x.astype(jnp.bfloat16)
    return jnp.concatenate([high, high], axis)


def dot(a, b):
    return jnp.dot(a, b, preferred_element_type=jnp.float32)


WIDE = 4
ROWS = 4


def columns(step):
    return pl.ds(pl.multiple_of(step * WIDE * R, WIDE * R), WIDE * R)


def first_section(load, mat_ref, start_ref, step_ref, out_ref):
    def one(step, carry):
        wr, wi = carry
        flat = dot(mat_ref[...], load(step))
        for part in range(WIDE):
            piece = flat[:, part * R : (part + 1) * R]
            re, im = turn(piece[:P1], piece[P1:], wr, wi)
            where = pl.ds(step * WIDE + part, P1, stride=Q)
            out_ref[0, where, :] = re
            out_ref[1, where, :] = im
            wr, wi = turn(wr, wi, step_ref[0], step_ref[1])
        return wr, wi

    lax.fori_loop(0, Q // WIDE, one, (start_ref[0], start_ref[1]))


def middle(mat_ref, pieces):
    data = jnp.concatenate([x for piece in pieces for x in piece], 1)
    flat = dot(mat_ref[...], split(data, 0))
    done = []
    for part in range(len(pieces)):
        low = flat[:, 2 * part * R : (2 * part + 1) * R]
        high = flat[:, (2 * part + 1) * R : (2 * part + 2) * R]
        done.append((low[:Q] - high[Q:], high[:Q] + low[Q:]))
    return done


def lanes(pieces):
    return jnp.concatenate([jnp.concatenate(piece, 1) for piece in pieces], 0)


def later_sections(cut, src_ref, step, second_ref, third_ref, outer_ref):
    pieces = []
    for part in range(ROWS):
        where = pl.ds(pl.multiple_of((step * ROWS + part) * Q, Q), Q)
        pieces.append((src_ref[0, where, :], src_ref[1, where, :]))
    pieces = middle(second_ref, pieces)
    pieces = [turn(re, im, outer_ref[0], outer_ref[1]) for re, im in pieces]
    return dot(cut(lanes(pieces), 1), third_ref[...])


def block(step):
    return pl.ds(pl.multiple_of(step * ROWS * Q, ROWS * Q), ROWS * Q)


def taps_kernel(
    taps_ref, mat_ref, start_ref, step_ref, second_ref, third_ref, outer_ref, out_ref, held, wide
):
    def widen(step, carry):
        where = pl.ds(pl.multiple_of(step * 512, 512), 512)
        wide[where, :] = taps_ref[where, :].astype(jnp.float32)
        return carry

    lax.fori_loop(0, HALF * Q // 512, widen, 0)

    def load(step):
        found = [wide[pl.ds(step * WIDE + part, HALF, stride=Q), :] for part in range(WIDE)]
        return twice(jnp.concatenate(found, 1), 0)

    first_section(load, mat_ref, start_ref, step_ref, held)

    def one(step, carry):
        flat = later_sections(split, held, step, second_ref, third_ref, outer_ref)
        out_ref[0, block(step), :] = flat[:, :R]
        out_ref[1, block(step), :] = flat[:, R:]
        return carry

    lax.fori_loop(0, P1 // ROWS, one, 0)


def signal_kernel(
    signal_ref,
    spectrum_ref,
    gain_ref,
    mat_ref,
    last_ref,
    start_ref,
    step_ref,
    second_ref,
    back_ref,
    third_ref,
    third_back_ref,
    outer_ref,
    out_ref,
    held,
    wide,
):
    sources, _, rows, _ = signal_ref.shape
    targets, _, span, _ = out_ref.shape

    def widen(step, carry):
        where = pl.ds(pl.multiple_of(step * rows, rows), rows)
        for part in range(2):
            wide[part, where, :] = signal_ref[step, part].astype(jnp.float32)
        return carry

    lax.fori_loop(0, sources, widen, 0)

    def digits(number):
        return pl.ds(number, HALF, stride=Q)

    def load(step):
        found = []
        for part in range(WIDE):
            where = digits(step * WIDE + part)
            found.append(jnp.concatenate([wide[0, where, :], wide[1, where, :]], 0))
        return twice(jnp.concatenate(found, 1), 0)

    first_section(load, mat_ref, start_ref, step_ref, held)

    def one(step, carry):
        flat = later_sections(twice, held, step, second_ref, third_ref, outer_ref)
        re, im = turn(
            flat[:, :R], flat[:, R:], spectrum_ref[0, block(step), :], spectrum_ref[1, block(step), :]
        )
        flat = dot(twice(jnp.concatenate([re, im], 1), 1), third_back_ref[...])
        pieces = []
        for part in range(ROWS):
            piece = flat[part * Q : (part + 1) * Q]
            pieces.append(turn(piece[:, :R], piece[:, R:], outer_ref[0], -outer_ref[1]))
        pieces = middle(back_ref, pieces)
        for part in range(ROWS):
            where = pl.ds(pl.multiple_of((step * ROWS + part) * Q, Q), Q)
            held[0, where, :] = pieces[part][0]
            held[1, where, :] = pieces[part][1]
        return carry

    lax.fori_loop(0, P1 // ROWS, one, 0)

    def finish(step, carry):
        wr, wi = carry
        found = []
        for part in range(WIDE):
            where = pl.ds(step * WIDE + part, P1, stride=Q)
            re, im = turn(held[0, where, :], held[1, where, :], wr, -wi)
            found.append(jnp.concatenate([re, im], 0))
            wr, wi = turn(wr, wi, step_ref[0], step_ref[1])
        flat = dot(last_ref[...], split(jnp.concatenate(found, 1), 0))
        for part in range(WIDE):
            where = digits(step * WIDE + part)
            for half in range(2):
                piece = flat[half * HALF : (half + 1) * HALF, part * R : (part + 1) * R]
                wide[half, where, :] = piece + gain_ref[half] * wide[half, where, :]
        return wr, wi

    lax.fori_loop(0, Q // WIDE, finish, (start_ref[0], start_ref[1]))

    def narrow(step, carry):
        where = pl.ds(pl.multiple_of(step * span, span), span)
        for part in range(2):
            out_ref[step, part] = wide[part, where, :].astype(jnp.bfloat16)
        return carry

    lax.fori_loop(0, targets, narrow, 0)


def product_kernel(keep_ref, key_ref, value_ref, out_ref, wide):
    pairs, _, _, sub, _ = out_ref.shape
    rows = 2 * pairs

    def one(step, carry):
        for part in range(8):
            at = step * 8 + part
            where = pl.ds(pl.multiple_of(at * R, R), R)
            keep = keep_ref[at].astype(jnp.float32)
            found = key_ref[:, where].astype(jnp.float32) * value_ref[:, where].astype(jnp.float32)
            wide[pl.ds(at, rows, stride=sub), :] = found * keep
        return carry

    lax.fori_loop(0, sub // 8, one, 0)
    for row in range(rows):
        out_ref[row // 2, 0, row % 2] = wide[row * sub : (row + 1) * sub, :].astype(jnp.bfloat16)


def multiply(keep, projected, chan, pairs):
    sub = keep.shape[0]
    here = sub * R

    def rows_of(which):
        return pl.BlockSpec((None, 2 * pairs, here), lambda at: (which, at, 0))

    return pl.pallas_call(
        product_kernel,
        grid=(chan,),
        out_shape=jax.ShapeDtypeStruct((pairs, chan, 2, sub, R), jnp.bfloat16),
        in_specs=[pl.BlockSpec(memory_space=pltpu.SMEM), rows_of(1), rows_of(2)],
        out_specs=pl.BlockSpec((pairs, 1, 2, sub, R), lambda at: (0, at, 0, 0, 0)),
        scratch_shapes=[pltpu.VMEM((2 * pairs * sub, R), jnp.float32)],
        compiler_params=pltpu.CompilerParams(vmem_limit_bytes=24 * 1024 * 1024),
        cost_estimate=pl.CostEstimate(
            flops=4 * chan * pairs * here, bytes_accessed=12 * chan * pairs * here, transcendentals=0
        ),
    )(keep, projected, projected)


def run(kernel, out_shape, out_dtype, flops, wide_shape, scalars, *operands):
    spaces = [pltpu.SMEM if at in scalars else pltpu.VMEM for at in range(len(operands))]
    return pl.pallas_call(
        kernel,
        out_shape=jax.ShapeDtypeStruct(out_shape, out_dtype),
        in_specs=[pl.BlockSpec(memory_space=space) for space in spaces],
        out_specs=pl.BlockSpec(memory_space=pltpu.VMEM),
        scratch_shapes=[
            pltpu.VMEM((2, P1 * Q, R), jnp.float32),
            pltpu.VMEM(wide_shape, jnp.float32),
        ],
        compiler_params=pltpu.CompilerParams(vmem_limit_bytes=52 * 1024 * 1024),
        cost_estimate=pl.CostEstimate(
            flops=flops, bytes_accessed=16 * 1024 * 1024, transcendentals=0
        ),
    )(*operands)


def transform_taps(taps, tabs):
    names = ("taps", "start", "step", "second", "third", "outer")
    return run(
        taps_kernel,
        (2, P1 * Q, R),
        jnp.float32,
        10**10,
        (HALF * Q, R),
        (),
        taps,
        *[tabs[name] for name in names],
    )


def convolve(signal, spectrum, gain, targets, tabs):
    names = (
        "first",
        "last",
        "start",
        "step",
        "second",
        "second_back",
        "third_short",
        "third_back",
        "outer",
    )
    operands = [tabs[name] for name in names]
    return run(
        signal_kernel,
        (targets, 2, HALF * Q // targets, R),
        jnp.bfloat16,
        2 * 10**10,
        (2, HALF * Q, R),
        (2,),
        signal,
        spectrum,
        gain,
        *operands,
    )


def body(projected, live_blocks, filters, skip_gain):
    seq, chan = lax.axis_size("seq"), lax.axis_size("chan")
    at_seq, at_chan = lax.axis_index("seq"), lax.axis_index("chan")
    channels, here = projected.shape[1], projected.shape[2]
    own = channels // chan
    pairs = own // 2
    copies = seq // pairs
    sub = live_blocks.shape[0] // chan
    span = here * chan
    keep = lax.dynamic_slice_in_dim(live_blocks, at_chan * sub, sub)
    rows = multiply(keep, projected, chan, pairs)
    rows = jnp.repeat(rows, copies, axis=0) if copies > 1 else rows
    rows = rows.reshape(seq * chan, 2, here // R, R)
    rows = lax.all_to_all(rows, ("seq", "chan"), split_axis=0, concat_axis=0, tiled=True)
    taps = filters.astype(jnp.bfloat16).reshape(span // R, R)
    taps = lax.all_gather(taps, "seq", axis=0, tiled=True)
    gate = lax.all_to_all(projected[0], "chan", split_axis=0, concat_axis=1, tiled=True)
    tabs = {name: jnp.asarray(table) for name, table in tables().items()}
    spectrum = transform_taps(taps, tabs)
    gain = lax.dynamic_slice_in_dim(skip_gain, 2 * (at_seq // copies), 2)
    summed = convolve(rows, spectrum, gain, seq, tabs)
    summed = lax.all_to_all(summed, "seq", split_axis=0, concat_axis=0, tiled=True)
    summed = summed[::copies].reshape(own, span)
    return (gate.astype(jnp.float32) * summed.astype(jnp.float32)).astype(jnp.bfloat16)


def solution(mesh):
    in_specs = (P(None, None, ("seq", "chan")), P("seq"), P("chan", "seq"), P("chan"))
    out_specs = P("chan", "seq")
    return jax.shard_map(body, mesh=mesh, in_specs=in_specs, out_specs=out_specs, check_vma=False)
```

```python
import math

import jax
import jax.numpy as jnp
import numpy as np
from jax import lax
from jax.experimental import pallas as pl
from jax.experimental.pallas import tpu as pltpu
from jax.sharding import PartitionSpec as P

P1 = 128
HALF = 64
Q = 64
R = 128
N = P1 * Q * R


def roots(exponent, total):
    angles = 2.0 * math.pi / total * (np.asarray(exponent, np.int64) % total)
    return np.cos(angles), -np.sin(angles)


def halves(matrix):
    high = np.asarray(matrix, np.float32).astype(jnp.bfloat16)
    low = (np.asarray(matrix) - high.astype(np.float64)).astype(jnp.bfloat16)
    return high, low


def thrice(matrix, axis):
    high, low = halves(matrix)
    return np.concatenate([high, high, low], axis)


def tables():
    k1, n1 = np.arange(P1), np.arange(HALF)
    k2, n3 = np.arange(Q), np.arange(R)
    fr, fi = roots(np.outer(k1, n1), P1)
    sr, si = roots(np.outer(k2, k2), Q)
    cr, ci = roots(np.outer(n3, n3), R)
    ar, ai = roots(np.outer(k1, n3), N)
    gr, gi = roots(np.outer(k1, np.ones(R, np.int64)), P1 * Q)
    br, bi = roots(np.outer(k2, n3), Q * R)
    return {
        "first": np.concatenate(halves(np.block([[fr, -fi], [fi, fr]])), 1),
        "taps": np.concatenate(halves(np.concatenate([fr, fi], 0)), 1),
        "last": thrice(np.block([[fr.T, fi.T], [-fi.T, fr.T]]) / N, 1),
        "second": thrice(np.concatenate([sr, si], 0), 1),
        "second_back": thrice(np.concatenate([sr, -si], 0), 1),
        "third": thrice(np.block([[cr, ci], [-ci, cr]]), 0),
        "third_short": np.concatenate(halves(np.block([[cr, ci], [-ci, cr]])), 0),
        "third_back": np.concatenate(halves(np.block([[cr, -ci], [ci, cr]])), 0),
        "start": np.stack([ar, ai]).astype(np.float32),
        "step": np.stack([gr, gi]).astype(np.float32),
        "outer": np.stack([br, bi]).astype(np.float32),
    }


def turn(re, im, c, s):
    return re * c - im * s, re * s + im * c


def split(x, axis):
    high = x.astype(jnp.bfloat16)
    low = (x - high.astype(jnp.float32)).astype(jnp.bfloat16)
    return jnp.concatenate([high, low, high], axis)


def twice(x, axis):
    high = x.astype(jnp.bfloat16)
    return jnp.concatenate([high, high], axis)


def dot(a, b):
    return jnp.dot(a, b, preferred_element_type=jnp.float32)


WIDE = 8
ROWS = 8


def columns(step):
    return pl.ds(pl.multiple_of(step * WIDE * R, WIDE * R), WIDE * R)


def first_section(load, mat_ref, start_ref, step_ref, out_ref):
    def one(step, carry):
        wr, wi = carry
        flat = dot(mat_ref[...], load(step))
        for part in range(WIDE):
            piece = flat[:, part * R : (part + 1) * R]
            re, im = turn(piece[:P1], piece[P1:], wr, wi)
            where = pl.ds(step * WIDE + part, P1, stride=Q)
            out_ref[0, where, :] = re
            out_ref[1, where, :] = im
            wr, wi = turn(wr, wi, step_ref[0], step_ref[1])
        return wr, wi

    lax.fori_loop(0, Q // WIDE, one, (start_ref[0], start_ref[1]))


def middle(mat_ref, pieces):
    data = jnp.concatenate([x for piece in pieces for x in piece], 1)
    flat = dot(mat_ref[...], split(data, 0))
    done = []
    for part in range(len(pieces)):
        low = flat[:, 2 * part * R : (2 * part + 1) * R]
        high = flat[:, (2 * part + 1) * R : (2 * part + 2) * R]
        done.append((low[:Q] - high[Q:], high[:Q] + low[Q:]))
    return done


def lanes(pieces):
    return jnp.concatenate([jnp.concatenate(piece, 1) for piece in pieces], 0)


def later_sections(cut, src_ref, step, second_ref, third_ref, outer_ref):
    pieces = []
    for part in range(ROWS):
        where = pl.ds(pl.multiple_of((step * ROWS + part) * Q, Q), Q)
        pieces.append((src_ref[0, where, :], src_ref[1, where, :]))
    pieces = middle(second_ref, pieces)
    pieces = [turn(re, im, outer_ref[0], outer_ref[1]) for re, im in pieces]
    return dot(cut(lanes(pieces), 1), third_ref[...])


def block(step):
    return pl.ds(pl.multiple_of(step * ROWS * Q, ROWS * Q), ROWS * Q)


def taps_kernel(
    taps_ref, mat_ref, start_ref, step_ref, second_ref, third_ref, outer_ref, out_ref, held, wide
):
    def widen(step, carry):
        where = pl.ds(pl.multiple_of(step * 512, 512), 512)
        wide[where, :] = taps_ref[where, :].astype(jnp.float32)
        return carry

    lax.fori_loop(0, HALF * Q // 512, widen, 0)

    def load(step):
        found = [wide[pl.ds(step * WIDE + part, HALF, stride=Q), :] for part in range(WIDE)]
        return twice(jnp.concatenate(found, 1), 0)

    first_section(load, mat_ref, start_ref, step_ref, held)

    def one(step, carry):
        flat = later_sections(split, held, step, second_ref, third_ref, outer_ref)
        out_ref[0, block(step), :] = flat[:, :R]
        out_ref[1, block(step), :] = flat[:, R:]
        return carry

    lax.fori_loop(0, P1 // ROWS, one, 0)


def signal_kernel(
    signal_ref,
    spectrum_ref,
    gain_ref,
    mat_ref,
    last_ref,
    start_ref,
    step_ref,
    second_ref,
    back_ref,
    third_ref,
    third_back_ref,
    outer_ref,
    out_ref,
    held,
    wide,
):
    sources, _, rows, _ = signal_ref.shape
    targets, _, span, _ = out_ref.shape

    def widen(step, carry):
        where = pl.ds(pl.multiple_of(step * rows, rows), rows)
        for part in range(2):
            wide[part, where, :] = signal_ref[step, part].astype(jnp.float32)
        return carry

    lax.fori_loop(0, sources, widen, 0)

    def digits(number):
        return pl.ds(number, HALF, stride=Q)

    def load(step):
        found = []
        for part in range(WIDE):
            where = digits(step * WIDE + part)
            found.append(jnp.concatenate([wide[0, where, :], wide[1, where, :]], 0))
        return twice(jnp.concatenate(found, 1), 0)

    first_section(load, mat_ref, start_ref, step_ref, held)

    def one(step, carry):
        flat = later_sections(twice, held, step, second_ref, third_ref, outer_ref)
        re, im = turn(
            flat[:, :R], flat[:, R:], spectrum_ref[0, block(step), :], spectrum_ref[1, block(step), :]
        )
        flat = dot(twice(jnp.concatenate([re, im], 1), 1), third_back_ref[...])
        pieces = []
        for part in range(ROWS):
            piece = flat[part * Q : (part + 1) * Q]
            pieces.append(turn(piece[:, :R], piece[:, R:], outer_ref[0], -outer_ref[1]))
        pieces = middle(back_ref, pieces)
        for part in range(ROWS):
            where = pl.ds(pl.multiple_of((step * ROWS + part) * Q, Q), Q)
            held[0, where, :] = pieces[part][0]
            held[1, where, :] = pieces[part][1]
        return carry

    lax.fori_loop(0, P1 // ROWS, one, 0)

    def finish(step, carry):
        wr, wi = carry
        found = []
        for part in range(WIDE):
            where = pl.ds(step * WIDE + part, P1, stride=Q)
            re, im = turn(held[0, where, :], held[1, where, :], wr, -wi)
            found.append(jnp.concatenate([re, im], 0))
            wr, wi = turn(wr, wi, step_ref[0], step_ref[1])
        flat = dot(last_ref[...], split(jnp.concatenate(found, 1), 0))
        for part in range(WIDE):
            where = digits(step * WIDE + part)
            for half in range(2):
                piece = flat[half * HALF : (half + 1) * HALF, part * R : (part + 1) * R]
                wide[half, where, :] = piece + gain_ref[half] * wide[half, where, :]
        return wr, wi

    lax.fori_loop(0, Q // WIDE, finish, (start_ref[0], start_ref[1]))

    def narrow(step, carry):
        where = pl.ds(pl.multiple_of(step * span, span), span)
        for part in range(2):
            out_ref[step, part] = wide[part, where, :].astype(jnp.bfloat16)
        return carry

    lax.fori_loop(0, targets, narrow, 0)


def product_kernel(keep_ref, key_ref, value_ref, out_ref, wide):
    pairs, _, _, sub, _ = out_ref.shape
    rows = 2 * pairs

    def one(step, carry):
        for part in range(8):
            at = step * 8 + part
            where = pl.ds(pl.multiple_of(at * R, R), R)
            keep = keep_ref[at].astype(jnp.float32)
            found = key_ref[:, where].astype(jnp.float32) * value_ref[:, where].astype(jnp.float32)
            wide[pl.ds(at, rows, stride=sub), :] = found * keep
        return carry

    lax.fori_loop(0, sub // 8, one, 0)
    for row in range(rows):
        out_ref[row // 2, 0, row % 2] = wide[row * sub : (row + 1) * sub, :].astype(jnp.bfloat16)


def multiply(keep, projected, chan, pairs):
    sub = keep.shape[0]
    here = sub * R

    def rows_of(which):
        return pl.BlockSpec((None, 2 * pairs, here), lambda at: (which, at, 0))

    return pl.pallas_call(
        product_kernel,
        grid=(chan,),
        out_shape=jax.ShapeDtypeStruct((pairs, chan, 2, sub, R), jnp.bfloat16),
        in_specs=[pl.BlockSpec(memory_space=pltpu.SMEM), rows_of(1), rows_of(2)],
        out_specs=pl.BlockSpec((pairs, 1, 2, sub, R), lambda at: (0, at, 0, 0, 0)),
        scratch_shapes=[pltpu.VMEM((2 * pairs * sub, R), jnp.float32)],
        compiler_params=pltpu.CompilerParams(vmem_limit_bytes=24 * 1024 * 1024),
        cost_estimate=pl.CostEstimate(
            flops=4 * chan * pairs * here, bytes_accessed=12 * chan * pairs * here, transcendentals=0
        ),
    )(keep, projected, projected)


def follow_kernel(value_ref, earlier_ref, out_ref):
    del value_ref, earlier_ref, out_ref


def follow(value, earlier):
    return pl.pallas_call(
        follow_kernel,
        out_shape=jax.ShapeDtypeStruct(value.shape, value.dtype),
        in_specs=[pl.BlockSpec(memory_space=pl.ANY)] * 2,
        out_specs=pl.BlockSpec(memory_space=pl.ANY),
        input_output_aliases={0: 0},
    )(value, earlier)


def gate_kernel(gate_ref, summed_ref, out_ref, wide):
    pairs, _, sub, _ = summed_ref.shape
    rows = 2 * pairs
    for row in range(rows):
        wide[row * sub : (row + 1) * sub, :] = summed_ref[row // 2, row % 2].astype(jnp.float32)

    def one(step, carry):
        for part in range(8):
            at = step * 8 + part
            where = pl.ds(pl.multiple_of(at * R, R), R)
            found = gate_ref[:, where].astype(jnp.float32) * wide[pl.ds(at, rows, stride=sub), :]
            out_ref[:, where] = found.astype(jnp.bfloat16)
        return carry

    lax.fori_loop(0, sub // 8, one, 0)


def apply_gate(gate, summed):
    chan, own, here = gate.shape
    pairs, sub = summed.shape[0], here // R
    return pl.pallas_call(
        gate_kernel,
        grid=(chan,),
        out_shape=jax.ShapeDtypeStruct((own, chan * here), jnp.bfloat16),
        in_specs=[
            pl.BlockSpec((None, own, here), lambda at: (at, 0, 0)),
            pl.BlockSpec((pairs, 2, sub, R), lambda at: (0, 0, at, 0)),
        ],
        out_specs=pl.BlockSpec((own, here), lambda at: (0, at)),
        scratch_shapes=[pltpu.VMEM((own * sub, R), jnp.float32)],
        compiler_params=pltpu.CompilerParams(vmem_limit_bytes=24 * 1024 * 1024),
        cost_estimate=pl.CostEstimate(
            flops=2 * chan * own * here, bytes_accessed=6 * chan * own * here, transcendentals=0
        ),
    )(gate, summed)


def run(kernel, out_shape, out_dtype, flops, wide_shape, scalars, *operands):
    spaces = [pltpu.SMEM if at in scalars else pltpu.VMEM for at in range(len(operands))]
    return pl.pallas_call(
        kernel,
        out_shape=jax.ShapeDtypeStruct(out_shape, out_dtype),
        in_specs=[pl.BlockSpec(memory_space=space) for space in spaces],
        out_specs=pl.BlockSpec(memory_space=pltpu.VMEM),
        scratch_shapes=[
            pltpu.VMEM((2, P1 * Q, R), jnp.float32),
            pltpu.VMEM(wide_shape, jnp.float32),
        ],
        compiler_params=pltpu.CompilerParams(vmem_limit_bytes=52 * 1024 * 1024),
        cost_estimate=pl.CostEstimate(
            flops=flops, bytes_accessed=16 * 1024 * 1024, transcendentals=0
        ),
    )(*operands)


def transform_taps(taps, tabs):
    names = ("taps", "start", "step", "second", "third", "outer")
    return run(
        taps_kernel,
        (2, P1 * Q, R),
        jnp.float32,
        10**10,
        (HALF * Q, R),
        (),
        taps,
        *[tabs[name] for name in names],
    )


def convolve(signal, spectrum, gain, targets, tabs):
    names = (
        "first",
        "last",
        "start",
        "step",
        "second",
        "second_back",
        "third_short",
        "third_back",
        "outer",
    )
    operands = [tabs[name] for name in names]
    return run(
        signal_kernel,
        (targets, 2, HALF * Q // targets, R),
        jnp.bfloat16,
        2 * 10**10,
        (2, HALF * Q, R),
        (2,),
        signal,
        spectrum,
        gain,
        *operands,
    )


def body(projected, live_blocks, filters, skip_gain):
    seq, chan = lax.axis_size("seq"), lax.axis_size("chan")
    at_seq, at_chan = lax.axis_index("seq"), lax.axis_index("chan")
    channels, here = projected.shape[1], projected.shape[2]
    own = channels // chan
    pairs = own // 2
    copies = seq // pairs
    sub = live_blocks.shape[0] // chan
    span = here * chan
    keep = lax.dynamic_slice_in_dim(live_blocks, at_chan * sub, sub)
    rows = multiply(keep, projected, chan, pairs)
    rows = jnp.repeat(rows, copies, axis=0) if copies > 1 else rows
    rows = rows.reshape(seq * chan, 2, here // R, R)
    taps = filters.astype(jnp.bfloat16).reshape(span // R, R)
    taps = lax.all_gather(taps, "seq", axis=0, tiled=True)
    rows = follow(rows, taps)
    rows = lax.all_to_all(rows, ("seq", "chan"), split_axis=0, concat_axis=0, tiled=True)
    gate = lax.all_to_all(
        projected[0].reshape(chan, own, here), "chan", split_axis=0, concat_axis=0, tiled=True
    )
    tabs = {name: jnp.asarray(table) for name, table in tables().items()}
    spectrum = transform_taps(taps, tabs)
    gain = lax.dynamic_slice_in_dim(skip_gain, 2 * (at_seq // copies), 2)
    summed = convolve(rows, spectrum, gain, seq, tabs)
    summed = lax.all_to_all(summed, "seq", split_axis=0, concat_axis=0, tiled=True)
    return apply_gate(gate, summed[::copies])


def solution(mesh):
    in_specs = (P(None, None, ("seq", "chan")), P("seq"), P("chan", "seq"), P("chan"))
    out_specs = P("chan", "seq")
    return jax.shard_map(body, mesh=mesh, in_specs=in_specs, out_specs=out_specs, check_vma=False)
```

```python
import math

import jax
import jax.numpy as jnp
import numpy as np
from jax import lax
from jax.experimental import pallas as pl
from jax.experimental.pallas import tpu as pltpu
from jax.sharding import PartitionSpec as P

P1 = 128
HALF = 64
Q = 64
R = 128
N = P1 * Q * R


def roots(exponent, total):
    angles = 2.0 * math.pi / total * (np.asarray(exponent, np.int64) % total)
    return np.cos(angles), -np.sin(angles)


def halves(matrix):
    high = np.asarray(matrix, np.float32).astype(jnp.bfloat16)
    low = (np.asarray(matrix) - high.astype(np.float64)).astype(jnp.bfloat16)
    return high, low


def thrice(matrix, axis):
    high, low = halves(matrix)
    return np.concatenate([high, high, low], axis)


def tables():
    k1, n1 = np.arange(P1), np.arange(HALF)
    k2, n3 = np.arange(Q), np.arange(R)
    fr, fi = roots(np.outer(k1, n1), P1)
    sr, si = roots(np.outer(k2, k2), Q)
    cr, ci = roots(np.outer(n3, n3), R)
    ar, ai = roots(np.outer(k1, n3), N)
    gr, gi = roots(np.outer(k1, np.ones(R, np.int64)), P1 * Q)
    br, bi = roots(np.outer(k2, n3), Q * R)
    return {
        "first": np.concatenate(halves(np.block([[fr, -fi], [fi, fr]])), 1),
        "taps": np.concatenate(halves(np.concatenate([fr, fi], 0)), 1),
        "last": thrice(np.block([[fr.T, fi.T], [-fi.T, fr.T]]) / N, 1),
        "second": thrice(np.concatenate([sr, si], 0), 1),
        "second_back": thrice(np.concatenate([sr, -si], 0), 1),
        "third": thrice(np.block([[cr, ci], [-ci, cr]]), 0),
        "third_short": np.concatenate(halves(np.block([[cr, ci], [-ci, cr]])), 0),
        "third_back": np.concatenate(halves(np.block([[cr, -ci], [ci, cr]])), 0),
        "start": np.stack([ar, ai]).astype(np.float32),
        "step": np.stack([gr, gi]).astype(np.float32),
        "outer": np.stack([br, bi]).astype(np.float32),
    }


def turn(re, im, c, s):
    return re * c - im * s, re * s + im * c


def split(x, axis):
    high = x.astype(jnp.bfloat16)
    low = (x - high.astype(jnp.float32)).astype(jnp.bfloat16)
    return jnp.concatenate([high, low, high], axis)


def twice(x, axis):
    high = x.astype(jnp.bfloat16)
    return jnp.concatenate([high, high], axis)


def dot(a, b):
    return jnp.dot(a, b, preferred_element_type=jnp.float32)


WIDE = 16
ROWS = 16


def columns(step):
    return pl.ds(pl.multiple_of(step * WIDE * R, WIDE * R), WIDE * R)


def first_section(load, mat_ref, start_ref, step_ref, out_ref):
    def one(step, carry):
        wr, wi = carry
        flat = dot(mat_ref[...], load(step))
        for part in range(WIDE):
            piece = flat[:, part * R : (part + 1) * R]
            re, im = turn(piece[:P1], piece[P1:], wr, wi)
            where = pl.ds(step * WIDE + part, P1, stride=Q)
            out_ref[0, where, :] = re
            out_ref[1, where, :] = im
            wr, wi = turn(wr, wi, step_ref[0], step_ref[1])
        return wr, wi

    lax.fori_loop(0, Q // WIDE, one, (start_ref[0], start_ref[1]))


def middle(mat_ref, pieces):
    data = jnp.concatenate([x for piece in pieces for x in piece], 1)
    flat = dot(mat_ref[...], split(data, 0))
    done = []
    for part in range(len(pieces)):
        low = flat[:, 2 * part * R : (2 * part + 1) * R]
        high = flat[:, (2 * part + 1) * R : (2 * part + 2) * R]
        done.append((low[:Q] - high[Q:], high[:Q] + low[Q:]))
    return done


def lanes(pieces):
    return jnp.concatenate([jnp.concatenate(piece, 1) for piece in pieces], 0)


def later_sections(cut, src_ref, step, second_ref, third_ref, outer_ref):
    pieces = []
    for part in range(ROWS):
        where = pl.ds(pl.multiple_of((step * ROWS + part) * Q, Q), Q)
        pieces.append((src_ref[0, where, :], src_ref[1, where, :]))
    pieces = middle(second_ref, pieces)
    pieces = [turn(re, im, outer_ref[0], outer_ref[1]) for re, im in pieces]
    return dot(cut(lanes(pieces), 1), third_ref[...])


def block(step):
    return pl.ds(pl.multiple_of(step * ROWS * Q, ROWS * Q), ROWS * Q)


def taps_kernel(
    taps_ref, mat_ref, start_ref, step_ref, second_ref, third_ref, outer_ref, out_ref, held, wide
):
    def widen(step, carry):
        where = pl.ds(pl.multiple_of(step * 512, 512), 512)
        wide[where, :] = taps_ref[where, :].astype(jnp.float32)
        return carry

    lax.fori_loop(0, HALF * Q // 512, widen, 0)

    def load(step):
        found = [wide[pl.ds(step * WIDE + part, HALF, stride=Q), :] for part in range(WIDE)]
        return twice(jnp.concatenate(found, 1), 0)

    first_section(load, mat_ref, start_ref, step_ref, held)

    def one(step, carry):
        flat = later_sections(split, held, step, second_ref, third_ref, outer_ref)
        out_ref[0, block(step), :] = flat[:, :R]
        out_ref[1, block(step), :] = flat[:, R:]
        return carry

    lax.fori_loop(0, P1 // ROWS, one, 0)


def signal_kernel(
    even_ref,
    odd_ref,
    spectrum_ref,
    gain_ref,
    mat_ref,
    last_ref,
    start_ref,
    step_ref,
    second_ref,
    back_ref,
    third_ref,
    third_back_ref,
    outer_ref,
    out_ref,
    held,
    wide,
):
    sources, rows, _ = even_ref.shape
    targets, _, span, _ = out_ref.shape

    def widen(step, carry):
        where = pl.ds(pl.multiple_of(step * rows, rows), rows)
        wide[0, where, :] = even_ref[step].astype(jnp.float32)
        wide[1, where, :] = odd_ref[step].astype(jnp.float32)
        return carry

    lax.fori_loop(0, sources, widen, 0)

    def digits(number):
        return pl.ds(number, HALF, stride=Q)

    def load(step):
        found = []
        for part in range(WIDE):
            where = digits(step * WIDE + part)
            found.append(jnp.concatenate([wide[0, where, :], wide[1, where, :]], 0))
        return twice(jnp.concatenate(found, 1), 0)

    first_section(load, mat_ref, start_ref, step_ref, held)

    def one(step, carry):
        flat = later_sections(twice, held, step, second_ref, third_ref, outer_ref)
        re, im = turn(
            flat[:, :R], flat[:, R:], spectrum_ref[0, block(step), :], spectrum_ref[1, block(step), :]
        )
        flat = dot(twice(jnp.concatenate([re, im], 1), 1), third_back_ref[...])
        pieces = []
        for part in range(ROWS):
            piece = flat[part * Q : (part + 1) * Q]
            pieces.append(turn(piece[:, :R], piece[:, R:], outer_ref[0], -outer_ref[1]))
        pieces = middle(back_ref, pieces)
        for part in range(ROWS):
            where = pl.ds(pl.multiple_of((step * ROWS + part) * Q, Q), Q)
            held[0, where, :] = pieces[part][0]
            held[1, where, :] = pieces[part][1]
        return carry

    lax.fori_loop(0, P1 // ROWS, one, 0)

    def finish(step, carry):
        wr, wi = carry
        found = []
        for part in range(WIDE):
            where = pl.ds(step * WIDE + part, P1, stride=Q)
            re, im = turn(held[0, where, :], held[1, where, :], wr, -wi)
            found.append(jnp.concatenate([re, im], 0))
            wr, wi = turn(wr, wi, step_ref[0], step_ref[1])
        flat = dot(last_ref[...], split(jnp.concatenate(found, 1), 0))
        for part in range(WIDE):
            where = digits(step * WIDE + part)
            for half in range(2):
                piece = flat[half * HALF : (half + 1) * HALF, part * R : (part + 1) * R]
                wide[half, where, :] = piece + gain_ref[half] * wide[half, where, :]
        return wr, wi

    lax.fori_loop(0, Q // WIDE, finish, (start_ref[0], start_ref[1]))

    def narrow(step, carry):
        where = pl.ds(pl.multiple_of(step * span, span), span)
        for part in range(2):
            out_ref[step, part] = wide[part, where, :].astype(jnp.bfloat16)
        return carry

    lax.fori_loop(0, targets, narrow, 0)


def product_kernel(keep_ref, key_ref, value_ref, even_ref, odd_ref, wide):
    pairs, _, sub, _ = even_ref.shape
    rows = 2 * pairs

    def one(step, carry):
        for part in range(8):
            at = step * 8 + part
            where = pl.ds(pl.multiple_of(at * R, R), R)
            keep = keep_ref[at].astype(jnp.float32)
            found = key_ref[:, where].astype(jnp.float32) * value_ref[:, where].astype(jnp.float32)
            wide[pl.ds(at, rows, stride=sub), :] = found * keep
        return carry

    lax.fori_loop(0, sub // 8, one, 0)
    for row in range(rows):
        out_ref = odd_ref if row % 2 else even_ref
        out_ref[row // 2, 0] = wide[row * sub : (row + 1) * sub, :].astype(jnp.bfloat16)


def multiply(keep, projected, chan, pairs):
    sub = keep.shape[0]
    here = sub * R

    def rows_of(which):
        return pl.BlockSpec((None, 2 * pairs, here), lambda at: (which, at, 0))

    return pl.pallas_call(
        product_kernel,
        grid=(chan,),
        out_shape=[jax.ShapeDtypeStruct((pairs, chan, sub, R), jnp.bfloat16)] * 2,
        in_specs=[pl.BlockSpec(memory_space=pltpu.SMEM), rows_of(1), rows_of(2)],
        out_specs=[pl.BlockSpec((pairs, 1, sub, R), lambda at: (0, at, 0, 0))] * 2,
        scratch_shapes=[pltpu.VMEM((2 * pairs * sub, R), jnp.float32)],
        compiler_params=pltpu.CompilerParams(vmem_limit_bytes=24 * 1024 * 1024),
        cost_estimate=pl.CostEstimate(
            flops=4 * chan * pairs * here, bytes_accessed=12 * chan * pairs * here, transcendentals=0
        ),
    )(keep, projected, projected)


def follow_kernel(value_ref, earlier_ref, out_ref):
    del value_ref, earlier_ref, out_ref


def follow(value, earlier):
    return pl.pallas_call(
        follow_kernel,
        out_shape=jax.ShapeDtypeStruct(value.shape, value.dtype),
        in_specs=[pl.BlockSpec(memory_space=pl.ANY)] * 2,
        out_specs=pl.BlockSpec(memory_space=pl.ANY),
        input_output_aliases={0: 0},
    )(value, earlier)


def gate_kernel(gate_ref, summed_ref, out_ref, wide):
    pairs, _, sub, _ = summed_ref.shape
    rows = 2 * pairs
    for row in range(rows):
        wide[row * sub : (row + 1) * sub, :] = summed_ref[row // 2, row % 2].astype(jnp.float32)

    def one(step, carry):
        for part in range(8):
            at = step * 8 + part
            where = pl.ds(pl.multiple_of(at * R, R), R)
            found = gate_ref[:, where].astype(jnp.float32) * wide[pl.ds(at, rows, stride=sub), :]
            out_ref[:, where] = found.astype(jnp.bfloat16)
        return carry

    lax.fori_loop(0, sub // 8, one, 0)


def apply_gate(gate, summed):
    chan, own, here = gate.shape
    pairs, sub = summed.shape[0], here // R
    return pl.pallas_call(
        gate_kernel,
        grid=(chan,),
        out_shape=jax.ShapeDtypeStruct((own, chan * here), jnp.bfloat16),
        in_specs=[
            pl.BlockSpec((None, own, here), lambda at: (at, 0, 0)),
            pl.BlockSpec((pairs, 2, sub, R), lambda at: (0, 0, at, 0)),
        ],
        out_specs=pl.BlockSpec((own, here), lambda at: (0, at)),
        scratch_shapes=[pltpu.VMEM((own * sub, R), jnp.float32)],
        compiler_params=pltpu.CompilerParams(vmem_limit_bytes=24 * 1024 * 1024),
        cost_estimate=pl.CostEstimate(
            flops=2 * chan * own * here, bytes_accessed=6 * chan * own * here, transcendentals=0
        ),
    )(gate, summed)


def run(kernel, out_shape, out_dtype, flops, wide_shape, scalars, *operands):
    spaces = [pltpu.SMEM if at in scalars else pltpu.VMEM for at in range(len(operands))]
    return pl.pallas_call(
        kernel,
        out_shape=jax.ShapeDtypeStruct(out_shape, out_dtype),
        in_specs=[pl.BlockSpec(memory_space=space) for space in spaces],
        out_specs=pl.BlockSpec(memory_space=pltpu.VMEM),
        scratch_shapes=[
            pltpu.VMEM((2, P1 * Q, R), jnp.float32),
            pltpu.VMEM(wide_shape, jnp.float32),
        ],
        compiler_params=pltpu.CompilerParams(vmem_limit_bytes=52 * 1024 * 1024),
        cost_estimate=pl.CostEstimate(
            flops=flops, bytes_accessed=16 * 1024 * 1024, transcendentals=0
        ),
    )(*operands)


def transform_taps(taps, tabs):
    names = ("taps", "start", "step", "second", "third", "outer")
    return run(
        taps_kernel,
        (2, P1 * Q, R),
        jnp.float32,
        10**10,
        (HALF * Q, R),
        (),
        taps,
        *[tabs[name] for name in names],
    )


def convolve(even, odd, spectrum, gain, targets, tabs):
    names = (
        "first",
        "last",
        "start",
        "step",
        "second",
        "second_back",
        "third_short",
        "third_back",
        "outer",
    )
    operands = [tabs[name] for name in names]
    return run(
        signal_kernel,
        (targets, 2, HALF * Q // targets, R),
        jnp.bfloat16,
        2 * 10**10,
        (2, HALF * Q, R),
        (3,),
        even,
        odd,
        spectrum,
        gain,
        *operands,
    )


def body(projected, live_blocks, filters, skip_gain):
    seq, chan = lax.axis_size("seq"), lax.axis_size("chan")
    at_seq, at_chan = lax.axis_index("seq"), lax.axis_index("chan")
    channels, here = projected.shape[1], projected.shape[2]
    own = channels // chan
    pairs = own // 2
    copies = seq // pairs
    sub = live_blocks.shape[0] // chan
    span = here * chan
    keep = lax.dynamic_slice_in_dim(live_blocks, at_chan * sub, sub)
    halves_of = multiply(keep, projected, chan, pairs)
    if copies > 1:
        halves_of = [jnp.repeat(rows, copies, axis=0) for rows in halves_of]
    even, odd = [rows.reshape(seq * chan, here // R, R) for rows in halves_of]
    taps = filters.astype(jnp.bfloat16).reshape(span // R, R)
    taps = lax.all_gather(taps, "seq", axis=0, tiled=True)
    odd = follow(odd, taps)
    even = lax.all_to_all(even, ("seq", "chan"), split_axis=0, concat_axis=0, tiled=True)
    odd = lax.all_to_all(odd, ("seq", "chan"), split_axis=0, concat_axis=0, tiled=True)
    gate = lax.all_to_all(
        projected[0].reshape(chan, own, here), "chan", split_axis=0, concat_axis=0, tiled=True
    )
    tabs = {name: jnp.asarray(table) for name, table in tables().items()}
    spectrum = transform_taps(taps, tabs)
    gain = lax.dynamic_slice_in_dim(skip_gain, 2 * (at_seq // copies), 2)
    summed = convolve(even, odd, spectrum, gain, seq, tabs)
    summed = lax.all_to_all(summed, "seq", split_axis=0, concat_axis=0, tiled=True)
    return apply_gate(gate, summed[::copies])


def solution(mesh):
    in_specs = (P(None, None, ("seq", "chan")), P("seq"), P("chan", "seq"), P("chan"))
    out_specs = P("chan", "seq")
    return jax.shard_map(body, mesh=mesh, in_specs=in_specs, out_specs=out_specs, check_vma=False)
```

```python
import math

import jax
import jax.numpy as jnp
import numpy as np
from jax import lax
from jax.experimental import pallas as pl
from jax.experimental.pallas import tpu as pltpu
from jax.sharding import PartitionSpec as P

P1 = 128
HALF = 64
Q = 64
R = 128
N = P1 * Q * R


def roots(exponent, total):
    angles = 2.0 * math.pi / total * (np.asarray(exponent, np.int64) % total)
    return np.cos(angles), -np.sin(angles)


def halves(matrix):
    high = np.asarray(matrix, np.float32).astype(jnp.bfloat16)
    low = (np.asarray(matrix) - high.astype(np.float64)).astype(jnp.bfloat16)
    return high, low


def thrice(matrix, axis):
    high, low = halves(matrix)
    return np.concatenate([high, high, low], axis)


def tables():
    k1, n1 = np.arange(P1), np.arange(HALF)
    k2, n3 = np.arange(Q), np.arange(R)
    fr, fi = roots(np.outer(k1, n1), P1)
    sr, si = roots(np.outer(k2, k2), Q)
    cr, ci = roots(np.outer(n3, n3), R)
    ar, ai = roots(np.outer(k1, n3), N)
    gr, gi = roots(np.outer(k1, np.ones(R, np.int64)), P1 * Q)
    br, bi = roots(np.outer(k2, n3), Q * R)
    return {
        "first": np.concatenate(halves(np.block([[fr, -fi], [fi, fr]])), 1),
        "taps": np.concatenate(halves(np.concatenate([fr, fi], 0)), 1),
        "last": thrice(np.block([[fr.T, fi.T], [-fi.T, fr.T]]) / N, 1),
        "second": thrice(np.concatenate([sr, si], 0), 1),
        "second_back": thrice(np.concatenate([sr, -si], 0), 1),
        "third": thrice(np.block([[cr, ci], [-ci, cr]]), 0),
        "third_short": np.concatenate(halves(np.block([[cr, ci], [-ci, cr]])), 0),
        "third_back": np.concatenate(halves(np.block([[cr, -ci], [ci, cr]])), 0),
        "start": np.stack([ar, ai]).astype(np.float32),
        "step": np.stack([gr, gi]).astype(np.float32),
        "outer": np.stack([br, bi]).astype(np.float32),
    }


def turn(re, im, c, s):
    return re * c - im * s, re * s + im * c


def split(x, axis):
    high = x.astype(jnp.bfloat16)
    low = (x - high.astype(jnp.float32)).astype(jnp.bfloat16)
    return jnp.concatenate([high, low, high], axis)


def twice(x, axis):
    high = x.astype(jnp.bfloat16)
    return jnp.concatenate([high, high], axis)


def dot(a, b):
    return jnp.dot(a, b, preferred_element_type=jnp.float32)


WIDE = 16
ROWS = 16


def columns(step):
    return pl.ds(pl.multiple_of(step * WIDE * R, WIDE * R), WIDE * R)


def first_section(load, mat_ref, start_ref, step_ref, out_ref):
    def one(step, carry):
        wr, wi = carry
        flat = dot(mat_ref[...], load(step))
        for part in range(WIDE):
            piece = flat[:, part * R : (part + 1) * R]
            re, im = turn(piece[:P1], piece[P1:], wr, wi)
            where = pl.ds(step * WIDE + part, P1, stride=Q)
            out_ref[0, where, :] = re
            out_ref[1, where, :] = im
            wr, wi = turn(wr, wi, step_ref[0], step_ref[1])
        return wr, wi

    lax.fori_loop(0, Q // WIDE, one, (start_ref[0], start_ref[1]))


def middle(mat_ref, pieces):
    data = jnp.concatenate([x for piece in pieces for x in piece], 1)
    flat = dot(mat_ref[...], split(data, 0))
    done = []
    for part in range(len(pieces)):
        low = flat[:, 2 * part * R : (2 * part + 1) * R]
        high = flat[:, (2 * part + 1) * R : (2 * part + 2) * R]
        done.append((low[:Q] - high[Q:], high[:Q] + low[Q:]))
    return done


def lanes(pieces):
    return jnp.concatenate([jnp.concatenate(piece, 1) for piece in pieces], 0)


def later_sections(cut, src_ref, step, second_ref, third_ref, outer_ref):
    pieces = []
    for part in range(ROWS):
        where = pl.ds(pl.multiple_of((step * ROWS + part) * Q, Q), Q)
        pieces.append((src_ref[0, where, :], src_ref[1, where, :]))
    pieces = middle(second_ref, pieces)
    pieces = [turn(re, im, outer_ref[0], outer_ref[1]) for re, im in pieces]
    return dot(cut(lanes(pieces), 1), third_ref[...])


def block(step):
    return pl.ds(pl.multiple_of(step * ROWS * Q, ROWS * Q), ROWS * Q)


def taps_kernel(
    taps_ref, mat_ref, start_ref, step_ref, second_ref, third_ref, outer_ref, out_ref, held, wide
):
    def widen(step, carry):
        where = pl.ds(pl.multiple_of(step * 512, 512), 512)
        wide[where, :] = taps_ref[where, :].astype(jnp.float32)
        return carry

    lax.fori_loop(0, HALF * Q // 512, widen, 0)

    def load(step):
        found = [wide[pl.ds(step * WIDE + part, HALF, stride=Q), :] for part in range(WIDE)]
        return twice(jnp.concatenate(found, 1), 0)

    first_section(load, mat_ref, start_ref, step_ref, held)

    def one(step, carry):
        flat = later_sections(split, held, step, second_ref, third_ref, outer_ref)
        out_ref[0, block(step), :] = flat[:, :R]
        out_ref[1, block(step), :] = flat[:, R:]
        return carry

    lax.fori_loop(0, P1 // ROWS, one, 0)


def signal_kernel(
    even_ref,
    odd_ref,
    spectrum_ref,
    gain_ref,
    mat_ref,
    last_ref,
    start_ref,
    step_ref,
    second_ref,
    back_ref,
    third_ref,
    third_back_ref,
    outer_ref,
    out_ref,
    held,
    wide,
):
    sources, rows, _ = even_ref.shape
    targets, _, span, _ = out_ref.shape

    def widen(step, carry):
        where = pl.ds(pl.multiple_of(step * rows, rows), rows)
        wide[0, where, :] = even_ref[step].astype(jnp.float32)
        wide[1, where, :] = odd_ref[step].astype(jnp.float32)
        return carry

    lax.fori_loop(0, sources, widen, 0)

    def digits(number):
        return pl.ds(number, HALF, stride=Q)

    def load(step):
        found = []
        for part in range(WIDE):
            where = digits(step * WIDE + part)
            found.append(jnp.concatenate([wide[0, where, :], wide[1, where, :]], 0))
        return twice(jnp.concatenate(found, 1), 0)

    first_section(load, mat_ref, start_ref, step_ref, held)

    def one(step, carry):
        flat = later_sections(twice, held, step, second_ref, third_ref, outer_ref)
        re, im = turn(
            flat[:, :R], flat[:, R:], spectrum_ref[0, block(step), :], spectrum_ref[1, block(step), :]
        )
        flat = dot(twice(jnp.concatenate([re, im], 1), 1), third_back_ref[...])
        pieces = []
        for part in range(ROWS):
            piece = flat[part * Q : (part + 1) * Q]
            pieces.append(turn(piece[:, :R], piece[:, R:], outer_ref[0], -outer_ref[1]))
        pieces = middle(back_ref, pieces)
        for part in range(ROWS):
            where = pl.ds(pl.multiple_of((step * ROWS + part) * Q, Q), Q)
            held[0, where, :] = pieces[part][0]
            held[1, where, :] = pieces[part][1]
        return carry

    lax.fori_loop(0, P1 // ROWS, one, 0)

    def finish(step, carry):
        wr, wi = carry
        found = []
        for part in range(WIDE):
            where = pl.ds(step * WIDE + part, P1, stride=Q)
            re, im = turn(held[0, where, :], held[1, where, :], wr, -wi)
            found.append(jnp.concatenate([re, im], 0))
            wr, wi = turn(wr, wi, step_ref[0], step_ref[1])
        flat = dot(last_ref[...], split(jnp.concatenate(found, 1), 0))
        for part in range(WIDE):
            where = digits(step * WIDE + part)
            for half in range(2):
                piece = flat[half * HALF : (half + 1) * HALF, part * R : (part + 1) * R]
                wide[half, where, :] = piece + gain_ref[half] * wide[half, where, :]
        return wr, wi

    lax.fori_loop(0, Q // WIDE, finish, (start_ref[0], start_ref[1]))

    def narrow(step, carry):
        where = pl.ds(pl.multiple_of(step * span, span), span)
        for part in range(2):
            out_ref[step, part] = wide[part, where, :].astype(jnp.bfloat16)
        return carry

    lax.fori_loop(0, targets, narrow, 0)


def product_kernel(keep_ref, key_ref, value_ref, _, even_ref, odd_ref, wide):
    pairs, sub = even_ref.shape[0], even_ref.shape[2]
    rows = 2 * pairs

    def one(step, carry):
        for part in range(8):
            at = step * 8 + part
            where = pl.ds(pl.multiple_of(at * R, R), R)
            keep = keep_ref[at].astype(jnp.float32)
            found = key_ref[:, where].astype(jnp.float32) * value_ref[:, where].astype(jnp.float32)
            wide[pl.ds(at, rows, stride=sub), :] = found * keep
        return carry

    lax.fori_loop(0, sub // 8, one, 0)
    for row in range(rows):
        out_ref = odd_ref if row % 2 else even_ref
        out_ref[row // 2, 0] = wide[row * sub : (row + 1) * sub, :].astype(jnp.bfloat16)


def multiply(keep, projected, earlier, chan, pairs):
    sub = keep.shape[0]
    here = sub * R

    def rows_of(which):
        return pl.BlockSpec((None, 2 * pairs, here), lambda at: (which, at, 0))

    return pl.pallas_call(
        product_kernel,
        grid=(chan,),
        out_shape=[jax.ShapeDtypeStruct((pairs, chan, sub, R), jnp.bfloat16)] * 2,
        in_specs=[
            pl.BlockSpec(memory_space=pltpu.SMEM),
            rows_of(1),
            rows_of(2),
            pl.BlockSpec(memory_space=pl.ANY),
        ],
        out_specs=[pl.BlockSpec((pairs, 1, sub, R), lambda at: (0, at, 0, 0))] * 2,
        scratch_shapes=[pltpu.VMEM((2 * pairs * sub, R), jnp.float32)],
        compiler_params=pltpu.CompilerParams(vmem_limit_bytes=24 * 1024 * 1024),
        cost_estimate=pl.CostEstimate(
            flops=4 * chan * pairs * here, bytes_accessed=12 * chan * pairs * here, transcendentals=0
        ),
    )(keep, projected, projected, earlier)


def follow_kernel(*refs):
    del refs


def follow(value, *earlier):
    return pl.pallas_call(
        follow_kernel,
        out_shape=jax.ShapeDtypeStruct(value.shape, value.dtype),
        in_specs=[pl.BlockSpec(memory_space=pl.ANY)] * (1 + len(earlier)),
        out_specs=pl.BlockSpec(memory_space=pl.ANY),
        input_output_aliases={0: 0},
    )(value, *earlier)


def gate_kernel(gate_ref, summed_ref, out_ref, wide):
    pairs, _, sub, _ = summed_ref.shape
    rows = 2 * pairs
    for row in range(rows):
        wide[row * sub : (row + 1) * sub, :] = summed_ref[row // 2, row % 2].astype(jnp.float32)

    def one(step, carry):
        for part in range(8):
            at = step * 8 + part
            where = pl.ds(pl.multiple_of(at * R, R), R)
            found = gate_ref[:, where].astype(jnp.float32) * wide[pl.ds(at, rows, stride=sub), :]
            out_ref[:, where] = found.astype(jnp.bfloat16)
        return carry

    lax.fori_loop(0, sub // 8, one, 0)


def apply_gate(gate, summed):
    chan, own, here = gate.shape
    pairs, sub = summed.shape[0], here // R
    return pl.pallas_call(
        gate_kernel,
        grid=(chan,),
        out_shape=jax.ShapeDtypeStruct((own, chan * here), jnp.bfloat16),
        in_specs=[
            pl.BlockSpec((None, own, here), lambda at: (at, 0, 0)),
            pl.BlockSpec((pairs, 2, sub, R), lambda at: (0, 0, at, 0)),
        ],
        out_specs=pl.BlockSpec((own, here), lambda at: (0, at)),
        scratch_shapes=[pltpu.VMEM((own * sub, R), jnp.float32)],
        compiler_params=pltpu.CompilerParams(vmem_limit_bytes=24 * 1024 * 1024),
        cost_estimate=pl.CostEstimate(
            flops=2 * chan * own * here, bytes_accessed=6 * chan * own * here, transcendentals=0
        ),
    )(gate, summed)


def run(kernel, out_shape, out_dtype, flops, wide_shape, scalars, *operands):
    spaces = [pltpu.SMEM if at in scalars else pltpu.VMEM for at in range(len(operands))]
    return pl.pallas_call(
        kernel,
        out_shape=jax.ShapeDtypeStruct(out_shape, out_dtype),
        in_specs=[pl.BlockSpec(memory_space=space) for space in spaces],
        out_specs=pl.BlockSpec(memory_space=pltpu.VMEM),
        scratch_shapes=[
            pltpu.VMEM((2, P1 * Q, R), jnp.float32),
            pltpu.VMEM(wide_shape, jnp.float32),
        ],
        compiler_params=pltpu.CompilerParams(vmem_limit_bytes=52 * 1024 * 1024),
        cost_estimate=pl.CostEstimate(
            flops=flops, bytes_accessed=16 * 1024 * 1024, transcendentals=0
        ),
    )(*operands)


def transform_taps(taps, tabs):
    names = ("taps", "start", "step", "second", "third", "outer")
    return run(
        taps_kernel,
        (2, P1 * Q, R),
        jnp.float32,
        10**10,
        (HALF * Q, R),
        (),
        taps,
        *[tabs[name] for name in names],
    )


def convolve(even, odd, spectrum, gain, targets, tabs):
    names = (
        "first",
        "last",
        "start",
        "step",
        "second",
        "second_back",
        "third_short",
        "third_back",
        "outer",
    )
    operands = [tabs[name] for name in names]
    return run(
        signal_kernel,
        (targets, 2, HALF * Q // targets, R),
        jnp.bfloat16,
        2 * 10**10,
        (2, HALF * Q, R),
        (3,),
        even,
        odd,
        spectrum,
        gain,
        *operands,
    )


def body(projected, live_blocks, filters, skip_gain):
    seq, chan = lax.axis_size("seq"), lax.axis_size("chan")
    at_seq, at_chan = lax.axis_index("seq"), lax.axis_index("chan")
    channels, here = projected.shape[1], projected.shape[2]
    own = channels // chan
    pairs = own // 2
    copies = seq // pairs
    sub = live_blocks.shape[0] // chan
    span = here * chan
    keep = lax.dynamic_slice_in_dim(live_blocks, at_chan * sub, sub)
    taps = filters.astype(jnp.bfloat16).reshape(span // R, R)
    halves_of = multiply(keep, projected, taps, chan, pairs)
    if copies > 1:
        halves_of = [jnp.repeat(rows, copies, axis=0) for rows in halves_of]
    even, odd = [rows.reshape(seq * chan, here // R, R) for rows in halves_of]
    taps = lax.all_gather(taps, "seq", axis=0, tiled=True)
    gate = lax.all_to_all(
        projected[0].reshape(chan, own, here), "chan", split_axis=0, concat_axis=0, tiled=True
    )
    odd = follow(odd, taps, gate)
    even = lax.all_to_all(even, ("seq", "chan"), split_axis=0, concat_axis=0, tiled=True)
    odd = lax.all_to_all(odd, ("seq", "chan"), split_axis=0, concat_axis=0, tiled=True)
    tabs = {name: jnp.asarray(table) for name, table in tables().items()}
    spectrum = transform_taps(taps, tabs)
    gain = lax.dynamic_slice_in_dim(skip_gain, 2 * (at_seq // copies), 2)
    summed = convolve(even, odd, spectrum, gain, seq, tabs)
    summed = lax.all_to_all(summed, "seq", split_axis=0, concat_axis=0, tiled=True)
    return apply_gate(gate, summed[::copies])


def solution(mesh):
    in_specs = (P(None, None, ("seq", "chan")), P("seq"), P("chan", "seq"), P("chan"))
    out_specs = P("chan", "seq")
    return jax.shard_map(body, mesh=mesh, in_specs=in_specs, out_specs=out_specs, check_vma=False)
```
